768 devices in a mesh: tile: 96 (over z, x, core), rep: 8 (over y).
Axes of the slice: x: 4, y: 8, z: 12, core: 2. Of those that a mesh axis runs over, the one named last changes fastest.
Arguments:
- amps: bfloat16 [768, 8, 1920], P('tile', 'rep'), may hold values from -6 to 6
- cycle_w: bfloat16 [8, 1920, 98304], P('rep', None, 'tile'), may hold values from -0.125 to 0.125
- occ_irrep: int32 [8], P('rep'), may hold values from 0 to 7
- vir_irrep: int32 [1920], replicated, may hold values from 0 to 7
- col_irrep: int32 [98304], P('tile'), may hold values from 0 to 7
Outputs:
- residual: bfloat16 [768, 98304], P('rep', 'tile')
The draws below stay inside these ranges and needn't reach their ends.
All inputs are finite; a program needn't handle non-finite values.
Results may differ from the reference program's by a relative error of at most 0.017.
Values may be sent and summed in bfloat16 or wider, within the bound.
No kernel may reach another device: no remote copies, remote signals or barrier semaphores. Data moves between devices by JAX's collectives and lax.ppermute only.
A program may use at most 32 MiB of HBM per device.

```python
import jax
import jax.numpy as jnp
from jax import lax

V = 1920
K_DEV = 1
KO = 8
ROWS = 768
COLS = 98304
N_REP = 8


def plant(array, key, low, top_value):
    longest = array.shape.index(max(array.shape))
    spots = []
    for shift in (0, 1):
        where = [jax.random.randint(jax.random.fold_in(key, axis), (), 0, length) for axis, length in enumerate(array.shape)]
        where[longest] = (where[longest] + shift) % array.shape[longest]
        spots.append(tuple(where))
    return array.at[spots[0]].set(low).at[spots[1]].set(top_value)


def level_of(rng, extent, shards, smallest, high):
    loudness = 1.0
    for position, shards_of in shards:
        steps = jax.random.uniform(jax.random.fold_in(jax.random.fold_in(rng, 6), position), (shards_of,), jnp.float32, smallest / len(shards), high / len(shards))
        loudness = loudness * jnp.repeat(jnp.exp(steps), extent[position] // shards_of).reshape((-1,) + (1,) * (len(extent) - 1 - position))
    return loudness


def gaussian(rng, extent, spread, most, pieces=(), kind=jnp.bfloat16):
    drawn = spread * jax.random.normal(rng, extent, jnp.float32)
    if pieces:
        drawn = drawn * level_of(rng, extent, pieces, -0.22, 0.18)
    return jnp.clip(drawn, -most, most).astype(kind)


def setup_inputs(seed: int = 0) -> dict:
    keys = jax.random.split(jax.random.key(seed), 6)
    return {
        "amps": gaussian(keys[0], (ROWS, KO, V), 1.0, 6.0, ((0, 96), (1, 8))),
        "cycle_w": gaussian(keys[1], (KO, V, COLS), (KO * V // 8) ** -0.5, 0.125, ((0, 8), (2, 96))),
        "occ_irrep": plant(jax.random.randint(keys[2], (KO,), 0, 8), jax.random.fold_in(keys[2], 1), 0, 7).astype(jnp.int32),
        "vir_irrep": plant(jax.random.randint(keys[3], (V,), 0, 8), jax.random.fold_in(keys[3], 1), 0, 7).astype(jnp.int32),
        "col_irrep": plant(jax.random.randint(keys[4], (COLS,), 0, 8), jax.random.fold_in(keys[4], 1), 0, 7).astype(jnp.int32),
    }


def reference(amps, cycle_w, occ_irrep, vir_irrep, col_irrep):
    total = jnp.zeros((ROWS, COLS), jnp.float32)
    for group in range(N_REP):
        first = group * K_DEV
        occ_part = occ_irrep[first:first + K_DEV]
        pair_sym = jnp.bitwise_xor(occ_part[:, None], vir_irrep[None, :]).reshape(-1)
        allowed = pair_sym[:, None] == col_irrep[None, :]
        weights = cycle_w[first:first + K_DEV].reshape(K_DEV * V, COLS)
        masked = jnp.where(allowed, weights, jnp.zeros((), weights.dtype))
        panel = amps[:, first:first + K_DEV, :].reshape(ROWS, K_DEV * V)
        partial_value = jnp.dot(panel, masked, preferred_element_type=jnp.float32).astype(jnp.bfloat16)
        partial_value = lax.optimization_barrier(partial_value)
        total = total + partial_value.astype(jnp.float32)
    return total.astype(jnp.bfloat16)
```

```python
import jax
import jax.numpy as jnp
from jax import lax
from jax.sharding import Mesh, PartitionSpec as P

NZ, NX, NC, NY = 12, 4, 2, 8
F32 = jnp.float32
BF16 = jnp.bfloat16


def shift(array, axis, size, step):
    return lax.ppermute(array, axis, [(i, (i + step) % size) for i in range(size)])


def gather(block, axis, size):
    copies = jnp.broadcast_to(block[None], (size,) + block.shape)
    return lax.all_to_all(copies, axis, 0, 0, tiled=False)


def reduce_scatter(terms):
    y = lax.axis_index("y")
    rows = terms.shape[0] // NY
    half = terms.shape[1] // 2

    def chunk(d):
        return lax.dynamic_slice_in_dim(terms, ((d + NY) % NY) * rows, rows)

    far = chunk(y + 4)
    from_right = shift(jnp.concatenate([chunk(y - 3), chunk(y - 1)], 0), "y", NY, -1)
    from_left = shift(jnp.concatenate([chunk(y + 3), chunk(y + 1)], 0), "y", NY, 1)
    far_right = shift(far[:, :half], "y", NY, -2)
    far_left = shift(far[:, half:], "y", NY, 2)
    down = chunk(y - 2).astype(F32) + from_right[:rows].astype(F32)
    down = jnp.concatenate([down[:, :half] + far_right.astype(F32), down[:, half:]], 1).astype(BF16)
    up = chunk(y + 2).astype(F32) + from_left[:rows].astype(F32)
    up = jnp.concatenate([up[:, :half], up[:, half:] + far_left.astype(F32)], 1).astype(BF16)
    got_down = shift(down, "y", NY, -2)
    got_up = shift(up, "y", NY, 2)
    total = chunk(y).astype(F32) + from_right[rows:].astype(F32) + from_left[rows:].astype(F32)
    return (total + got_down.astype(F32) + got_up.astype(F32)).astype(BF16)


def on_device(amps, cycle_w, occ_irrep, vir_irrep, col_irrep):
    c = lax.axis_index("c")
    pair_sym = jnp.bitwise_xor(occ_irrep[:, None], vir_irrep[None, :]).reshape(-1)
    allowed = pair_sym[:, None] == col_irrep[None, :]
    weights = cycle_w.reshape(-1, cycle_w.shape[2])
    masked = lax.optimization_barrier(jnp.where(allowed, weights, jnp.zeros((), weights.dtype)))
    block = amps.reshape(amps.shape[0], -1)
    along_z = gather(block, "z", NZ)
    mine = gather(along_z, "x", NX).reshape(-1, block.shape[1])
    theirs = shift(mine, "c", NC, 1)

    def product(rows):
        return jnp.dot(rows, masked, preferred_element_type=F32).astype(BF16)

    here = product(mine).reshape(NX, NZ, amps.shape[0], -1)
    there = product(theirs).reshape(NX, NZ, amps.shape[0], -1)
    first = jnp.where(c == 0, here, there)
    second = jnp.where(c == 0, there, here)
    terms = jnp.stack([first, second], 2).transpose(1, 0, 2, 3, 4).reshape(-1, here.shape[-1])
    return reduce_scatter(terms)


def solution(mesh):
    fine = Mesh(mesh.devices.reshape(NZ, NX, NC, NY), ("z", "x", "c", "y"))
    tile = ("z", "x", "c")
    in_specs = (P(tile, "y", None), P("y", None, tile), P("y"), P(), P(tile))
    return jax.shard_map(
        on_device, mesh=fine, in_specs=in_specs, out_specs=P("y", tile), check_vma=False
    )
```

```python
import jax
import jax.numpy as jnp
from jax import lax
from jax.sharding import Mesh, PartitionSpec as P

ZH, ZL, NX, NC, NY = 6, 2, 4, 2, 8
F32 = jnp.float32
BF16 = jnp.bfloat16
tie = lax.optimization_barrier


def gather(block, axis, size):
    copies = jnp.broadcast_to(block[None], (size,) + block.shape)
    return lax.all_to_all(copies, axis, 0, 0, tiled=False)


def mirrored(array, step):
    pairs = []
    for c in range(NC):
        for y in range(NY):
            to = (y + (step if c == 0 else -step)) % NY
            pairs.append((c * NY + y, c * NY + to))
    return lax.ppermute(array, ("c", "y"), pairs)


def plus(*terms):
    total = terms[0].astype(F32)
    for term in terms[1:]:
        total = total + term.astype(F32)
    return total.astype(BF16)


def reduce_scatter(terms):
    y = lax.axis_index("y")
    sign = 1 - 2 * lax.axis_index("c")

    def part(offset):
        return lax.dynamic_index_in_dim(terms, (y + sign * offset + NY) % NY, 0, keepdims=False)

    near_down = mirrored(jnp.stack([part(-1), part(-3)]), -1)
    near_up = mirrored(jnp.stack([part(1), part(3)]), 1)
    far = mirrored(part(4), 2)
    down = plus(part(-2), near_down[1])
    got_down = mirrored(down, -2)
    up = plus(part(2), near_up[1], far)
    got_up = mirrored(up, 2)
    return plus(part(0), near_down[0], near_up[0], got_down, got_up)


def on_device(amps, cycle_w, occ_irrep, vir_irrep, col_irrep):
    c = lax.axis_index("c")
    pair_sym = jnp.bitwise_xor(occ_irrep[:, None], vir_irrep[None, :]).reshape(-1)
    allowed = pair_sym.astype(BF16)[:, None] == col_irrep.astype(BF16)[None, :]
    weights = cycle_w.reshape(-1, cycle_w.shape[2])
    block = amps.reshape(amps.shape[0], -1)
    along_z = gather(block, "zh", ZH)
    mine = gather(along_z, ("zl", "x"), ZL * NX)
    theirs = lax.ppermute(mine, "c", [(0, 1), (1, 0)])
    masked = tie(jnp.where(allowed, weights, jnp.zeros((), weights.dtype)))

    def product(rows):
        part = jnp.dot(rows.reshape(-1, rows.shape[-1]), masked, preferred_element_type=F32).astype(BF16)
        return part.reshape(ZL, NX, ZH, -1, part.shape[-1]).transpose(2, 0, 1, 3, 4)

    here = product(mine)
    there = product(theirs)
    first = jnp.where(c == 0, here, there)
    second = jnp.where(c == 0, there, here)
    terms = jnp.stack([first, second], 3).reshape(NY, -1, weights.shape[1])
    return reduce_scatter(terms)


def solution(mesh):
    fine = Mesh(mesh.devices.reshape(ZH, ZL, NX, NC, NY), ("zh", "zl", "x", "c", "y"))
    tile = ("zh", "zl", "x", "c")
    in_specs = (P(tile, "y", None), P("y", None, tile), P("y"), P(), P(tile))
    return jax.shard_map(
        on_device, mesh=fine, in_specs=in_specs, out_specs=P("y", tile), check_vma=False
    )
```

```python
import jax
import jax.numpy as jnp
from jax import lax
from jax.sharding import Mesh, PartitionSpec as P

ZH, ZL, NX, NC, NY = 6, 2, 4, 2, 8
F32 = jnp.float32
BF16 = jnp.bfloat16
tie = lax.optimization_barrier


def gather(block, axis, size):
    copies = jnp.broadcast_to(block[None], (size,) + block.shape)
    return lax.all_to_all(copies, axis, 0, 0, tiled=False)


def mirrored(array, step):
    pairs = []
    for c in range(NC):
        for y in range(NY):
            to = (y + (step if c == 0 else -step)) % NY
            pairs.append((c * NY + y, c * NY + to))
    return lax.ppermute(array, ("c", "y"), pairs)


def plus(*terms):
    total = terms[0].astype(F32)
    for term in terms[1:]:
        total = total + term.astype(F32)
    return total.astype(BF16)


def reduce_scatter(terms):
    y = lax.axis_index("y")
    sign = 1 - 2 * lax.axis_index("c")

    def part(offset):
        return lax.dynamic_index_in_dim(terms, (y + sign * offset + NY) % NY, 0, keepdims=False)

    part = dict(zip(range(-3, 5), tie(tuple(part(offset) for offset in range(-3, 5)))))
    far = mirrored(part[4], 1)
    near_down = mirrored(jnp.stack([part[-1], part[-3]]), -1)
    near_up = mirrored(jnp.stack([part[1], plus(part[3], far)]), 1)
    got_down = mirrored(plus(part[-2], near_down[1]), -2)
    got_up = mirrored(plus(part[2], near_up[1]), 2)
    return plus(part[0], near_down[0], near_up[0], got_down, got_up)


def on_device(amps, cycle_w, occ_irrep, vir_irrep, col_irrep):
    c = lax.axis_index("c")
    pair_sym = jnp.bitwise_xor(occ_irrep[:, None], vir_irrep[None, :]).reshape(-1)
    allowed = pair_sym.astype(BF16)[:, None] == col_irrep.astype(BF16)[None, :]
    weights = cycle_w.reshape(-1, cycle_w.shape[2])
    block = amps.reshape(amps.shape[0], -1)
    masked = jnp.where(allowed, weights, jnp.zeros((), weights.dtype))
    along_z, masked = tie((gather(block, "zh", ZH), masked))
    mine = gather(along_z, ("zl", "x"), ZL * NX)
    theirs = lax.ppermute(mine, "c", [(0, 1), (1, 0)])

    def product(rows):
        part = jnp.dot(rows.reshape(-1, rows.shape[-1]), masked, preferred_element_type=F32).astype(BF16)
        return part.reshape(ZL, NX, ZH, -1, part.shape[-1]).transpose(2, 0, 1, 3, 4)

    here = product(mine)
    there = product(theirs)
    first = jnp.where(c == 0, here, there)
    second = jnp.where(c == 0, there, here)
    terms = jnp.stack([first, second], 3).reshape(NY, -1, weights.shape[1])
    return reduce_scatter(terms)


def solution(mesh):
    fine = Mesh(mesh.devices.reshape(ZH, ZL, NX, NC, NY), ("zh", "zl", "x", "c", "y"))
    tile = ("zh", "zl", "x", "c")
    in_specs = (P(tile, "y", None), P("y", None, tile), P("y"), P(), P(tile))
    return jax.shard_map(
        on_device, mesh=fine, in_specs=in_specs, out_specs=P("y", tile), check_vma=False
    )
```

```python
import jax
import jax.numpy as jnp
from jax import lax
from jax.experimental import pallas as pl
from jax.experimental.pallas import tpu as pltpu
from jax.sharding import Mesh, PartitionSpec as P

ZH, ZL, NX, NC, NY = 6, 2, 4, 2, 8
F32 = jnp.float32
BF16 = jnp.bfloat16
tie = lax.optimization_barrier


def gather(block, axis, size):
    copies = jnp.broadcast_to(block[None], (size,) + block.shape)
    return lax.all_to_all(copies, axis, 0, 0, tiled=False)


ORDER = [5, 4, 0, 1, 2, 3]


def gather_z(block):
    copies = jnp.broadcast_to(block[None], (ZH,) + block.shape)
    got = lax.all_to_all(copies, "zh", 0, 0, tiled=False, axis_index_groups=[ORDER])
    return jnp.stack([got[ORDER.index(i)] for i in range(ZH)])


def mirrored(array, step):
    pairs = []
    for c in range(NC):
        for y in range(NY):
            to = (y + (step if c == 0 else -step)) % NY
            pairs.append((c * NY + y, c * NY + to))
    return lax.ppermute(array, ("c", "y"), pairs)


def plus(*terms):
    total = terms[0].astype(F32)
    for term in terms[1:]:
        total = total + term.astype(F32)
    return total.astype(BF16)


def reduce_scatter(terms):
    y = lax.axis_index("y")
    sign = 1 - 2 * lax.axis_index("c")

    def part(offset):
        return lax.dynamic_index_in_dim(terms, (y + sign * offset + NY) % NY, 0, keepdims=False)

    part = dict(zip(range(-3, 5), tie(tuple(part(offset) for offset in range(-3, 5)))))
    far = mirrored(part[4], 1)
    near_down = mirrored(jnp.stack([part[-1], part[-3]]), -1)
    near_up = mirrored(jnp.stack([part[1], plus(part[3], far)]), 1)
    got_down = mirrored(plus(part[-2], near_down[1]), -2)
    got_up = mirrored(plus(part[2], near_up[1]), 2)
    return plus(part[0], near_down[0], near_up[0], got_down, got_up)


def mask_rows(occ_ref, vir_ref, col_ref, weights_ref, out_ref):
    lanes = vir_ref.shape[-1]
    for i in range(weights_ref.shape[0] // lanes):
        sym = jnp.bitwise_xor(vir_ref[0, i:i + 1, :], occ_ref[0]).astype(F32)
        sym = jnp.broadcast_to(sym, (lanes, lanes)).T.astype(BF16)
        rows = pl.ds(i * lanes, lanes)
        for j in range(weights_ref.shape[1] // lanes):
            cols = pl.ds(j * lanes, lanes)
            allowed = sym == col_ref[j:j + 1, :].astype(F32).astype(BF16)
            out_ref[rows, cols] = jnp.where(allowed, weights_ref[rows, cols], jnp.zeros((), BF16))


def mask_weights(occ_irrep, vir_irrep, col_irrep, weights):
    steps, lanes = 5, 128
    depth, width = weights.shape
    return pl.pallas_call(
        mask_rows,
        out_shape=jax.ShapeDtypeStruct(weights.shape, weights.dtype),
        grid=(steps,),
        in_specs=[
            pl.BlockSpec(memory_space=pltpu.SMEM),
            pl.BlockSpec((1, depth // steps // lanes, lanes), lambda i: (i, 0, 0)),
            pl.BlockSpec((width // lanes, lanes), lambda i: (0, 0)),
            pl.BlockSpec((depth // steps, width), lambda i: (i, 0)),
        ],
        out_specs=pl.BlockSpec((depth // steps, width), lambda i: (i, 0)),
        compiler_params=pltpu.CompilerParams(vmem_limit_bytes=8 << 20),
        cost_estimate=pl.CostEstimate(flops=depth * width, bytes_accessed=4 * depth * width, transcendentals=0),
    )(occ_irrep, vir_irrep.reshape(steps, -1, lanes), col_irrep.reshape(-1, lanes), weights)


def on_device(amps, cycle_w, occ_irrep, vir_irrep, col_irrep):
    c = lax.axis_index("c")
    weights = cycle_w.reshape(-1, cycle_w.shape[2])
    block = amps.reshape(amps.shape[0], -1)
    masked = mask_weights(occ_irrep, vir_irrep, col_irrep, weights)
    mine, masked = tie((gather(gather_z(block), ("zl", "x"), ZL * NX), masked))
    theirs = lax.ppermute(mine, "c", [(0, 1), (1, 0)])

    def product(rows):
        part = jnp.dot(rows.reshape(-1, rows.shape[-1]), masked, preferred_element_type=F32).astype(BF16)
        return part.reshape(ZL, NX, ZH, -1, part.shape[-1]).transpose(2, 0, 1, 3, 4)

    here = product(mine)
    there = product(theirs)
    first = jnp.where(c == 0, here, there)
    second = jnp.where(c == 0, there, here)
    terms = jnp.stack([first, second], 3).reshape(NY, -1, weights.shape[1])
    return reduce_scatter(terms)


def solution(mesh):
    fine = Mesh(mesh.devices.reshape(ZH, ZL, NX, NC, NY), ("zh", "zl", "x", "c", "y"))
    tile = ("zh", "zl", "x", "c")
    in_specs = (P(tile, "y", None), P("y", None, tile), P("y"), P(), P(tile))
    return jax.shard_map(
        on_device, mesh=fine, in_specs=in_specs, out_specs=P("y", tile), check_vma=False
    )
```

```python
import jax
import jax.numpy as jnp
from jax import lax
from jax.experimental import pallas as pl
from jax.experimental.pallas import tpu as pltpu
from jax.sharding import Mesh, PartitionSpec as P

ZH, ZL, NX, NC, NY = 6, 2, 4, 2, 8
F32 = jnp.float32
BF16 = jnp.bfloat16
tie = lax.optimization_barrier


def gather(block, axis, size):
    copies = jnp.broadcast_to(block[None], (size,) + block.shape)
    return lax.all_to_all(copies, axis, 0, 0, tiled=False)


ORDER = [5, 4, 0, 1, 2, 3]


def gather_z(block):
    copies = jnp.broadcast_to(block[None], (ZH,) + block.shape)
    got = lax.all_to_all(copies, "zh", 0, 0, tiled=False, axis_index_groups=[ORDER])
    return jnp.stack([got[ORDER.index(i)] for i in range(ZH)])


def mirrored(array, step):
    pairs = []
    for c in range(NC):
        for y in range(NY):
            to = (y + (step if c == 0 else -step)) % NY
            pairs.append((c * NY + y, c * NY + to))
    return lax.ppermute(array, ("c", "y"), pairs)


def plus(*terms):
    total = terms[0].astype(F32)
    for term in terms[1:]:
        total = total + term.astype(F32)
    return total.astype(BF16)


def reduce_scatter(terms):
    y = lax.axis_index("y")
    sign = 1 - 2 * lax.axis_index("c")

    def part(offset):
        return lax.dynamic_index_in_dim(terms, (y + sign * offset + NY) % NY, 0, keepdims=False)

    part = dict(zip(range(-3, 5), tie(tuple(part(offset) for offset in range(-3, 5)))))
    far = mirrored(part[4], 1)
    near_down = mirrored(jnp.stack([part[-1], part[-3]]), -1)
    near_up = mirrored(jnp.stack([part[1], plus(part[3], far)]), 1)
    got_down = mirrored(plus(part[-2], near_down[1]), -2)
    got_up = mirrored(plus(part[2], near_up[1]), 2)
    return plus(part[0], near_down[0], near_up[0], got_down, got_up)


def mask_rows(occ_ref, vir_ref, col_ref, weights_ref, out_ref):
    lanes = vir_ref.shape[-1]
    for i in range(weights_ref.shape[0] // lanes):
        sym = jnp.bitwise_xor(vir_ref[0, i:i + 1, :], occ_ref[0]).astype(F32)
        sym = jnp.broadcast_to(sym, (lanes, lanes)).T.astype(BF16)
        rows = pl.ds(i * lanes, lanes)
        for j in range(weights_ref.shape[1] // lanes):
            cols = pl.ds(j * lanes, lanes)
            allowed = sym == col_ref[j:j + 1, :].astype(F32).astype(BF16)
            out_ref[rows, cols] = jnp.where(allowed, weights_ref[rows, cols], jnp.zeros((), BF16))


def mask_weights(occ_irrep, vir_irrep, col_irrep, weights):
    steps, lanes = 5, 128
    depth, width = weights.shape
    return pl.pallas_call(
        mask_rows,
        out_shape=pltpu.VMEM(weights.shape, weights.dtype),
        grid=(steps,),
        in_specs=[
            pl.BlockSpec(memory_space=pltpu.SMEM),
            pl.BlockSpec((1, depth // steps // lanes, lanes), lambda i: (i, 0, 0)),
            pl.BlockSpec((width // lanes, lanes), lambda i: (0, 0)),
            pl.BlockSpec((depth // steps, width), lambda i: (i, 0)),
        ],
        out_specs=pl.BlockSpec((depth // steps, width), lambda i: (i, 0)),
        compiler_params=pltpu.CompilerParams(vmem_limit_bytes=8 << 20),
        cost_estimate=pl.CostEstimate(flops=depth * width, bytes_accessed=4 * depth * width, transcendentals=0),
    )(occ_irrep, vir_irrep.reshape(steps, -1, lanes), col_irrep.reshape(-1, lanes), weights)


def on_device(amps, cycle_w, occ_irrep, vir_irrep, col_irrep):
    c = lax.axis_index("c")
    weights = cycle_w.reshape(-1, cycle_w.shape[2])
    block = amps.reshape(amps.shape[0], -1)
    masked = mask_weights(occ_irrep, vir_irrep, col_irrep, weights)
    mine, masked = tie((gather(gather_z(block), ("zl", "x"), ZL * NX), masked))
    theirs = lax.ppermute(mine, "c", [(0, 1), (1, 0)])

    def product(rows):
        part = jnp.dot(rows.reshape(-1, rows.shape[-1]), masked, preferred_element_type=F32).astype(BF16)
        return part.reshape(ZL, NX, ZH, -1, part.shape[-1]).transpose(2, 0, 1, 3, 4)

    here = product(mine)
    there = product(theirs)
    first = jnp.where(c == 0, here, there)
    second = jnp.where(c == 0, there, here)
    terms = jnp.stack([first, second], 3).reshape(NY, -1, weights.shape[1])
    return reduce_scatter(terms)


def solution(mesh):
    fine = Mesh(mesh.devices.reshape(ZH, ZL, NX, NC, NY), ("zh", "zl", "x", "c", "y"))
    tile = ("zh", "zl", "x", "c")
    in_specs = (P(tile, "y", None), P("y", None, tile), P("y"), P(), P(tile))
    return jax.shard_map(
        on_device, mesh=fine, in_specs=in_specs, out_specs=P("y", tile), check_vma=False
    )
```
